512 devices in a mesh: row: 4 (over x), col: 4 (over y), dep: 32 (over z, core).
Axes of the slice: x: 4, y: 4, z: 16, core: 2. Of those that a mesh axis runs over, the one named last changes fastest.
Arguments:
- labels: int32 [32, 64, 4096], P('row', 'col', 'dep'), may hold values from 0 to 7, as said below
- conductivity: float32 [8], replicated, may hold values from 0.001 to 20, as said below
Outputs:
- pressure: float32 [3, 32, 64, 4096], P(None, 'row', 'col', 'dep')
- permeability: float32 [3, 3], replicated
The draws below stay inside these ranges and needn't reach their ends.
Inputs may be any that keep to these rules, and one draw needn't show every extreme that they name: `labels`: each label is a phase index; phases are more frequent toward higher indices along each of the three dimensions. `conductivity`: conductivities are positive.
All inputs are finite; a program needn't handle non-finite values.
Results may differ from the reference program's by a relative error of at most 0.0003.
Values sent between devices are 32-bit elements; how exact they have to be, the bound alone decides.
No kernel may reach another device: no remote copies, remote signals or barrier semaphores. Data moves between devices by JAX's collectives and lax.ppermute only.
A program may use at most 64 MiB of HBM per device.

```python
import jax
import jax.numpy as jnp
from jax import lax

LEVELS = 4
COARSE = 6
PHASES = 8
NX = 32
NY = 64
NZ = 4096


def draw_labels(key, part):
    key = jax.random.fold_in(key, 11)
    shape_all = (NX, NY, NZ)
    baseline = jax.random.randint(key, shape_all, 0, PHASES - 3)
    coord_x = lax.broadcasted_iota(jnp.int32, shape_all, 0)
    coord_y = lax.broadcasted_iota(jnp.int32, shape_all, 1)
    coord_z = lax.broadcasted_iota(jnp.int32, shape_all, 2)
    gradient_bias = 2 * coord_x // NX + 2 * coord_y // NY + 2 * coord_z // NZ
    return (baseline + gradient_bias).astype(jnp.int32)


def draw_conductivity(key, part):
    key = jax.random.fold_in(key, 23)
    fraction = jnp.arange(PHASES, dtype=jnp.float32) / (PHASES - 1)
    spread_factor = jax.random.uniform(key, (PHASES,), jnp.float32, 0.7, 1.4)
    return (jnp.power(10.0, -2.5 + 3.5 * fraction) * spread_factor).astype(jnp.float32)


def setup_inputs(seed: int = 0) -> dict:
    seeds = jax.random.split(jax.random.key(seed), 3)
    return {
        "labels": draw_labels(jax.random.fold_in(seeds[2], 71), 0),
        "conductivity": draw_conductivity(jax.random.fold_in(seeds[2], 71), 0),
    }


RELAX_WEIGHT = 0.8


def cropped(field, margin):
    if margin == 0:
        return field
    return field[..., margin:-margin, margin:-margin, margin:-margin]


def shifted(field, axis_no, stride):
    ndims = field.ndim
    result = field
    for spatial in range(3):
        position = ndims - 3 + spatial
        extent = field.shape[position]
        begin = 1 + stride if spatial == axis_no else 1
        result = lax.slice_in_dim(result, begin, begin + extent - 2, axis=position)
    return result


def pad_zero(field):
    return jnp.pad(field, [(0, 0)] * (field.ndim - 3) + [(1, 1)] * 3)


def weights_of(padded_k, level_scale):
    centre = cropped(padded_k, 1)
    weights = []
    for axis_no in range(3):
        for stride in (1, -1):
            beside = shifted(padded_k, axis_no, stride)
            harmonic = 2.0 * centre * beside / (centre + beside)
            weights.append(jnp.where(beside > 0.0, harmonic, centre) * level_scale)
    centre_sum = weights[0]
    for weight in weights[1:]:
        centre_sum = centre_sum + weight
    return weights, centre_sum


def apply_op(padded, weights, centre_sum):
    summed = centre_sum * cropped(padded, 1)
    index = 0
    for axis_no in range(3):
        for stride in (1, -1):
            summed = summed - weights[index] * shifted(padded, axis_no, stride)
            index = index + 1
    return summed


def jacobi_sweep(padded, sources, weights, centre_sum):
    return cropped(padded, 1) + RELAX_WEIGHT * (sources - apply_op(padded, weights, centre_sum)) / centre_sum


def coarsen(field):
    leading = field.shape[:-3]
    size_x, size_y, size_z = field.shape[-3:]
    reshaped = field.reshape(leading + (size_x // 2, 2, size_y // 2, 2, size_z // 2, 2))
    count = len(leading)
    return jnp.mean(reshaped, axis=(count + 1, count + 3, count + 5))


def refine(field):
    for position in (-3, -2, -1):
        field = jnp.repeat(field, 2, axis=position)
    return field


def vcycle(sources, cell_conduct, level_no):
    weights, centre_sum = weights_of(pad_zero(cell_conduct), 0.25 ** level_no)
    iterate = RELAX_WEIGHT * sources / centre_sum
    if level_no == LEVELS - 1:
        for counter in range(COARSE - 1):
            iterate = jacobi_sweep(pad_zero(iterate), sources, weights, centre_sum)
        return iterate
    iterate = jacobi_sweep(pad_zero(iterate), sources, weights, centre_sum)
    remainder = sources - apply_op(pad_zero(iterate), weights, centre_sum)
    coarse_fix = vcycle(coarsen(remainder), coarsen(cell_conduct), level_no + 1)
    iterate = iterate + refine(coarse_fix)
    for counter in range(2):
        iterate = jacobi_sweep(pad_zero(iterate), sources, weights, centre_sum)
    return iterate


def reference(labels, conductivity):
    cell_conduct = conductivity[labels]
    weights, centre_sum = weights_of(pad_zero(cell_conduct), 1.0)
    sources = jnp.stack([weights[2 * solve_no + 1] - weights[2 * solve_no] for solve_no in range(3)])
    pressure = lax.map(lambda source: vcycle(source, cell_conduct, 0), sources)
    cell_count = pressure.shape[1] * pressure.shape[2] * pressure.shape[3]
    tensor_rows = []
    for axis_no in range(3):
        entries = []
        for solve_no in range(3):
            padded = pad_zero(pressure[solve_no])
            centre = cropped(padded, 1)
            unit_val = 1.0 if axis_no == solve_no else 0.0
            rising = shifted(padded, axis_no, 1) - centre + unit_val
            falling = centre - shifted(padded, axis_no, -1) + unit_val
            fluxes = 0.5 * (weights[2 * axis_no] * rising + weights[2 * axis_no + 1] * falling)
            entries.append(jnp.sum(fluxes))
        tensor_rows.append(jnp.stack(entries))
    permeability = jnp.stack(tensor_rows) / cell_count
    return pressure, permeability
```

```python
import jax
import jax.numpy as jnp
from jax import lax
from jax.experimental import pallas as pl
from jax.experimental.pallas import tpu as pltpu
from jax.sharding import PartitionSpec as P


RELAX = 0.8
LANES = 128
PAD = 8
HALO0 = 4
HALO1 = 40
OWN0 = 128
OWN1 = 64
NZ0 = OWN0 + 2 * HALO0
NZ1 = OWN1 + 2 * HALO1
NZ2 = NZ1 // 2
NZ3 = 40
VMEM_LIMIT = 56 * 1024 * 1024


def lanes_of(shape=(8, LANES)):
    return lax.broadcasted_iota(jnp.int32, shape, 1)


def turned(tile, amount):
    return pltpu.roll(tile, amount % LANES, 1)


def harmonic(a, b):
    return 2.0 * a * b / jnp.maximum(a + b, 1e-30)


def tiles(count):
    return range(0, count, 8)


def zero_pads(ref, lead, nz):
    zero = jnp.zeros((8, LANES), jnp.float32)
    for idx in lead:
        ref[(*idx, pl.ds(0, 8), slice(None))] = zero
        ref[(*idx, pl.ds(PAD + nz, 8), slice(None))] = zero


def wrap_rows(ref, lead, nx, nz):
    for idx in lead:
        for t in tiles(nz):
            rows = pl.ds(PAD + t, 8)
            ref[(*idx, 0, rows, slice(None))] = turned(ref[(*idx, nx, rows, slice(None))], 64)
            ref[(*idx, nx + 1, rows, slice(None))] = turned(ref[(*idx, 1, rows, slice(None))], 64)


def coefficients(k, wx, wy, wz, emit, level, nx, nz):
    step = 1 << level
    lane = lanes_of()
    low_half = lane < 64
    y_first = (lane % 64) < step
    y_last = (lane % 64) >= 64 - step
    zero = jnp.zeros((8, LANES), jnp.float32)
    for t in tiles(nz):
        rows = pl.ds(PAD + t, 8)
        k[0, rows, :] = jnp.where(low_half, 0.0, turned(k[nx, rows, :], 64))
        k[nx + 1, rows, :] = jnp.where(low_half, turned(k[1, rows, :], 64), 0.0)

    def faces(x, carry):
        wz[x, pl.ds(0, 8), :] = zero
        for t in tiles(nz):
            rows = pl.ds(PAD + t, 8)
            kc = k[x + 1, rows, :]
            wx[x + 1, rows, :] = harmonic(kc, k[x + 2, rows, :])
            wy[x, rows, :] = harmonic(kc, jnp.where(y_last, 0.0, turned(kc, -step)))
            wz[x, rows, :] = harmonic(kc, k[x + 1, pl.ds(PAD + t + 1, 8), :])
        return carry

    lax.fori_loop(0, nx, faces, 0)
    for t in tiles(nz):
        rows = pl.ds(PAD + t, 8)
        wx[0, rows, :] = turned(wx[nx, rows, :], 64)

    def cells(x, carry):
        for t in tiles(nz):
            rows = pl.ds(PAD + t, 8)
            kc = k[x + 1, rows, :]
            wyp = wy[x, rows, :]
            weights = [
                wx[x + 1, rows, :],
                wx[x, rows, :],
                wyp,
                turned(wyp, step),
                wz[x, rows, :],
                wz[x, pl.ds(PAD + t - 1, 8), :],
            ]
            outer = [
                k[x + 2, rows, :] == 0.0,
                k[x, rows, :] == 0.0,
                y_last,
                y_first,
                k[x + 1, pl.ds(PAD + t + 1, 8), :] == 0.0,
                k[x + 1, pl.ds(PAD + t - 1, 8), :] == 0.0,
            ]
            full = [jnp.where(o, kc, w) for o, w in zip(outer, weights)]
            total = full[0]
            for w in full[1:]:
                total = total + w
            total = jnp.where(kc > 0.0, total, 1.0)
            emit(x, t, kc, outer, weights, full, total)
        return carry

    lax.fori_loop(0, nx, cells, 0)


def neighbours(c, v, x, c0, v0row, step):
    coef = [c[n, x, pl.ds(c0, 8), :] for n in range(6)]
    centres, sums = [], []
    for f in range(3):
        vc = v[f, x + 1, pl.ds(v0row, 8), :]
        acc = coef[0] * v[f, x + 2, pl.ds(v0row, 8), :] + coef[1] * v[f, x, pl.ds(v0row, 8), :]
        acc = acc + (coef[2] * turned(vc, -step) + coef[3] * turned(vc, step))
        acc = acc + (
            coef[4] * v[f, x + 1, pl.ds(v0row + 1, 8), :] + coef[5] * v[f, x + 1, pl.ds(v0row - 1, 8), :]
        )
        centres.append(vc)
        sums.append(acc)
    return centres, sums


def sweep(c, v, first, out, level, nx, lo, hi):
    step = 1 << level

    def row(x, carry):
        for t in range(lo, hi, 8):
            centres, sums = neighbours(c, v, x, t, PAD + t, step)
            for f in range(3):
                out[f, x + 1, pl.ds(PAD + t, 8), :] = sums[f] + (
                    first[f, x, pl.ds(t, 8), :] + (1.0 - RELAX) * centres[f]
                )
        return carry

    lax.fori_loop(0, nx, row, 0)
    wrap_fields(out, nx, lo, hi)


def wrap_fields(v, nx, lo, hi):
    for f in range(3):
        for t in range(lo, hi, 8):
            rows = pl.ds(PAD + t, 8)
            v[f, 0, rows, :] = turned(v[f, nx, rows, :], 64)
            v[f, nx + 1, rows, :] = turned(v[f, 1, rows, :], 64)


def residual(c, v, first, invq, r, level, nx, nz):
    step = 1 << level

    def row(x, carry):
        for t in tiles(nz):
            centres, sums = neighbours(c, v, x, t, PAD + t, step)
            scale = invq[x, pl.ds(t, 8), :]
            for f in range(3):
                r[f, x, pl.ds(t, 8), :] = (
                    sums[f] + (first[f, x, pl.ds(t, 8), :] - RELAX * centres[f])
                ) * scale
        return carry

    lax.fori_loop(0, nx, row, 0)


def mean8(read, level):
    step = 1 << level
    total = (read(0, 0) + read(0, 1)) + (read(1, 0) + read(1, 1))
    upper = (lanes_of() // step) % 2 == 1
    mate = jnp.where(upper, turned(total, step), turned(total, -step))
    return (total + mate) * 0.125


def strided(start):
    return pl.ds(start, 8, stride=2)


def look_up(labels_ref, table_ref, out_ref):
    labels = labels_ref[...]
    k = jnp.zeros(labels.shape, jnp.float32)
    for phase in range(8):
        k = jnp.where(labels == phase, table_ref[phase], k)
    out_ref[...] = k.reshape(LANES, LANES).T


def down_kernel(blocks, c, v0, v1, g, own, low, high, diag, k, wx, wy, wz, invq, r, va, vb):
    lane = lanes_of()

    def place(t, carry):
        rows = pl.ds(pl.multiple_of(t * 8, 8), 8)
        for odd in range(2):
            held = [blocks[(2 * (g8 // 4) + odd) * 4 + g8 % 4, rows, :] for g8 in range(8)]
            for bit in range(3):
                dist = 1 << bit
                clear = (lane // (16 * dist)) % 2 == 0
                for i in range(8):
                    if not i & dist:
                        a, b = held[i], held[i + dist]
                        held[i] = jnp.where(clear, a, turned(b, 16 * dist))
                        held[i + dist] = jnp.where(clear, turned(a, -16 * dist), b)
            for x8 in range(8):
                k[odd * 8 + x8 + 1, pl.ds(pl.multiple_of(PAD + t * 8, 8), 8), :] = held[x8]
        return carry

    lax.fori_loop(0, NZ0 // 8, place, 0)
    zero_pads(k, [(x,) for x in range(18)], NZ0)
    zero_pads(va, [(f, x) for f in range(3) for x in range(18)], NZ0)
    zero_pads(vb, [(f, x) for f in range(3) for x in range(18)], NZ0)

    diag[...] = jnp.zeros_like(diag)
    zeros = jnp.zeros((8, LANES), jnp.float32)

    def emit(x, t, kc, outer, weights, full, total):
        rows = pl.ds(t, 8)
        q = RELAX / total
        for n in range(6):
            c[n, x, rows, :] = q * weights[n]
        invq[x, rows, :] = (1.0 / RELAX) * total
        depth = lax.broadcasted_iota(jnp.int32, (8, LANES), 0) + (t - HALO0)
        inside = (depth >= 0) & (depth < OWN0)
        for f in range(3):
            up, down = full[2 * f], full[2 * f + 1]
            first = q * (down - up)
            v0[f, x, rows, :] = first
            va[f, x + 1, pl.ds(PAD + t, 8), :] = first
            half_up = jnp.where(outer[2 * f], 0.5 * up, up)
            half_down = jnp.where(outer[2 * f + 1], 0.5 * down, down)
            g[f, x, rows, :] = half_down - half_up
            diag[f, :, :] = diag[f, :, :] + jnp.where(inside, 0.5 * (up + down), 0.0)

    coefficients(k, wx, wy, wz, emit, 0, 16, NZ0)
    wrap_fields(va, 16, 0, NZ0)
    sweep(c, va, v0, vb, 0, 16, 0, NZ0)
    residual(c, vb, v0, invq, r, 0, 16, NZ0)

    def save(x, carry):
        for f in range(3):
            for t in tiles(NZ0):
                v1[f, x, pl.ds(t, 8), :] = vb[f, x + 1, pl.ds(PAD + t, 8), :]
        return carry

    lax.fori_loop(0, 16, save, 0)

    def coarse(x, carry):
        for t in tiles(OWN1):
            for f in range(3):
                own[f, x, pl.ds(t, 8), :] = mean8(
                    lambda dx, dz: r[f, 2 * x + dx, strided(HALO0 + 2 * t + dz), :], 0
                )
            own[3, x, pl.ds(t, 8), :] = mean8(
                lambda dx, dz: k[2 * x + dx + 1, strided(PAD + HALO0 + 2 * t + dz), :], 0
            )
        even = lane % 2 == 0
        for ref, base in ((low, 0), (high, OWN1 - HALO1)):
            for t in tiles(HALO1):
                rows = pl.ds(base + t, 8)
                for pair in range(2):
                    ref[pair, x, pl.ds(t, 8), :] = jnp.where(
                        even, own[2 * pair, x, rows, :], own[2 * pair + 1, x, rows, :]
                    )
        return carry

    lax.fori_loop(0, 8, coarse, 0)


def up_kernel(
    where_ref, c0, v00, v01, g, own, below, above, diag,
    p, sums,
    k1, wx1, wy1, wz1, c1, f1, q1, r1, va1, vb1,
    k2, wx2, wy2, wz2, c2, f2, q2, r2, va2, vb2,
    k3, wx3, wy3, wz3, c3, f3, va3, vb3,
    wide1, wide2, wide3, va0, vb0, acc,
):
    lane = lanes_of()
    even = lane % 2 == 0

    def fill(x, carry):
        for t in tiles(OWN1):
            for f in range(3):
                f1[f, x, pl.ds(HALO1 + t, 8), :] = own[f, x, pl.ds(t, 8), :]
            k1[x + 1, pl.ds(PAD + HALO1 + t, 8), :] = own[3, x, pl.ds(t, 8), :]
        for ref, base in ((below, 0), (above, HALO1 + OWN1)):
            for t in tiles(HALO1):
                for pair in range(2):
                    packed = ref[pair, x, pl.ds(t, 8), :]
                    one = jnp.where(even, packed, turned(packed, 1))
                    two = jnp.where(even, turned(packed, -1), packed)
                    f1[2 * pair, x, pl.ds(base + t, 8), :] = one
                    if pair == 0:
                        f1[1, x, pl.ds(base + t, 8), :] = two
                    else:
                        k1[x + 1, pl.ds(PAD + base + t, 8), :] = two
        return carry

    lax.fori_loop(0, 8, fill, 0)

    def prepare(level, nx, nz, k, wx, wy, wz, c, first, invq, va, vb):
        zero_pads(k, [(x,) for x in range(nx + 2)], nz)
        zero_pads(va, [(f, x) for f in range(3) for x in range(nx + 2)], nz)
        zero_pads(vb, [(f, x) for f in range(3) for x in range(nx + 2)], nz)
        scale = 4.0**level

        def emit(x, t, kc, outer, weights, full, total):
            rows = pl.ds(t, 8)
            q = RELAX / total
            for n in range(6):
                c[n, x, rows, :] = q * weights[n]
            if invq is not None:
                invq[x, rows, :] = (1.0 / (RELAX * scale)) * total
            for f in range(3):
                start = (q * scale) * first[f, x, rows, :]
                first[f, x, rows, :] = start
                va[f, x + 1, pl.ds(PAD + t, 8), :] = start

        coefficients(k, wx, wy, wz, emit, level, nx, nz)
        wrap_fields(va, nx, 0, nz)

    def restrict(level, nx, nz, r, k, first, knext):
        def row(x, carry):
            for t in tiles(nz):
                for f in range(3):
                    first[f, x, pl.ds(t, 8), :] = mean8(
                        lambda dx, dz: r[f, 2 * x + dx, strided(2 * t + dz), :], level
                    )
                knext[x + 1, pl.ds(PAD + t, 8), :] = mean8(
                    lambda dx, dz: k[2 * x + dx + 1, strided(PAD + 2 * t + dz), :], level
                )
            return carry

        lax.fori_loop(0, nx, row, 0)

    def widen(e, wide, nx, first_row, count):
        def row(x, carry):
            for f in range(3):
                for t in tiles(count):
                    part = e[f, x + 1, pl.ds(PAD + first_row + t, 8), :]
                    wide[f, x, strided(2 * t), :] = part
                    wide[f, x, strided(2 * t + 1), :] = part
            return carry

        lax.fori_loop(0, nx, row, 0)

    def add_coarse(v, wide, nx, lo, hi, first_row):
        def row(x, carry):
            for f in range(3):
                for t in range(lo, hi, 8):
                    rows = pl.ds(PAD + t, 8)
                    v[f, x + 1, rows, :] = v[f, x + 1, rows, :] + wide[f, x // 2, pl.ds(t - first_row, 8), :]
            return carry

        lax.fori_loop(0, nx, row, 0)
        wrap_fields(v, nx, lo, hi)

    prepare(1, 8, NZ1, k1, wx1, wy1, wz1, c1, f1, q1, va1, vb1)
    sweep(c1, va1, f1, vb1, 1, 8, 0, NZ1)
    residual(c1, vb1, f1, q1, r1, 1, 8, NZ1)
    restrict(1, 4, NZ2, r1, k1, f2, k2)

    prepare(2, 4, NZ2, k2, wx2, wy2, wz2, c2, f2, q2, va2, vb2)
    sweep(c2, va2, f2, vb2, 2, 4, 0, NZ2)
    for f in range(3):
        for x in range(4):
            r2[f, x, pl.ds(NZ2, 8), :] = jnp.zeros((8, LANES), jnp.float32)
    residual(c2, vb2, f2, q2, r2, 2, 4, NZ2)
    restrict(2, 2, NZ3, r2, k2, f3, k3)

    prepare(3, 2, NZ3, k3, wx3, wy3, wz3, c3, f3, None, va3, vb3)
    sweep(c3, va3, f3, vb3, 3, 2, 0, NZ3)
    sweep(c3, vb3, f3, va3, 3, 2, 0, NZ3)
    sweep(c3, va3, f3, vb3, 3, 2, 0, NZ3)
    sweep(c3, vb3, f3, va3, 3, 2, 0, NZ3)
    sweep(c3, va3, f3, vb3, 3, 2, 0, NZ3)

    widen(vb3, wide3, 2, 0, NZ3)
    add_coarse(vb2, wide3, 4, 0, NZ2, 0)
    sweep(c2, vb2, f2, va2, 2, 4, 0, NZ2)
    sweep(c2, va2, f2, vb2, 2, 4, 0, NZ2)

    lo1, hi1 = HALO1 - 8, HALO1 + OWN1 + 8
    widen(vb2, wide2, 4, lo1 // 2, (hi1 - lo1) // 2)
    add_coarse(vb1, wide2, 8, lo1, hi1, lo1)
    sweep(c1, vb1, f1, va1, 1, 8, lo1, hi1)
    sweep(c1, va1, f1, vb1, 1, 8, lo1, hi1)

    widen(vb1, wide1, 8, HALO1 - HALO0 // 2, 72)
    zero_pads(va0, [(f, x) for f in range(3) for x in range(18)], NZ0)
    zero_pads(vb0, [(f, x) for f in range(3) for x in range(18)], NZ0)

    def add_first(x, carry):
        for f in range(3):
            for t in tiles(NZ0):
                va0[f, x + 1, pl.ds(PAD + t, 8), :] = (
                    v01[f, x, pl.ds(t, 8), :] + wide1[f, x // 2, pl.ds(t, 8), :]
                )
        return carry

    lax.fori_loop(0, 16, add_first, 0)
    wrap_fields(va0, 16, 0, NZ0)
    sweep(c0, va0, v00, vb0, 0, 16, 0, NZ0)

    acc[...] = jnp.zeros_like(acc)

    def last(x, carry):
        for t in tiles(OWN0):
            centres, near = neighbours(c0, vb0, x, HALO0 + t, PAD + HALO0 + t, 1)
            rows = pl.ds(HALO0 + t, 8)
            done = [
                near[f] + (v00[f, x, rows, :] + (1.0 - RELAX) * centres[f]) for f in range(3)
            ]
            for f in range(3):
                va0[f, x, pl.ds(t, 8), :] = done[f]
            for i in range(3):
                gi = g[i, x, rows, :]
                for j in range(3):
                    acc[3 * i + j, :, :] = acc[3 * i + j, :, :] + gi * done[j]
        return carry

    lax.fori_loop(0, 16, last, 0)

    flat = jnp.zeros((1, LANES), jnp.float32)
    one_row = lax.broadcasted_iota(jnp.int32, (1, LANES), 1)
    for i in range(3):
        for j in range(3):
            part = acc[3 * i + j, :, :]
            if i == j:
                part = part + diag[i, :, :]
            whole = jnp.sum(jnp.sum(part, axis=0, keepdims=True), axis=1, keepdims=True)
            flat = jnp.where(one_row == 3 * i + j, whole, flat)
    sums[...] = flat

    row_no, col_no = where_ref[0], where_ref[1]
    x_base = (row_no % 2) * 8
    lane_base = (row_no // 2) * 64 + col_no * 16
    wide_lane = lanes_of((OWN0, LANES))
    for f in range(3):
        block = jnp.zeros((OWN0, LANES), jnp.float32)
        for x8 in range(8):
            piece = va0[f, x_base + x8, pl.ds(0, OWN0), :]
            amount = lax.rem(x8 * 16 - lane_base + 2 * LANES, LANES)
            block = jnp.where(wide_lane // 16 == x8, pltpu.roll(piece, amount, 1), block)
        p[f, :, :] = block.T


def f32(*shape):
    return jax.ShapeDtypeStruct(shape, jnp.float32)


def scratch(*shape):
    return pltpu.VMEM(shape, jnp.float32)


def level_scratch(nx, nz, last=False):
    rows = nz + 2 * PAD
    got = [
        scratch(nx + 2, rows, LANES), scratch(nx + 1, rows, LANES), scratch(nx, rows, LANES),
        scratch(nx, rows, LANES), scratch(6, nx, nz, LANES), scratch(3, nx, nz, LANES),
    ]
    if not last:
        got += [scratch(nx, nz, LANES), scratch(3, nx, nz + 8, LANES)]
    return got + [scratch(3, nx + 2, rows, LANES)] * 2


def params():
    return pltpu.CompilerParams(vmem_limit_bytes=VMEM_LIMIT)


VM = pl.BlockSpec(memory_space=pltpu.VMEM)
SM = pl.BlockSpec(memory_space=pltpu.SMEM)


def conductivities(labels, table):
    return pl.pallas_call(
        look_up, out_shape=f32(LANES, LANES), in_specs=[VM, SM], out_specs=VM, name="look_up"
    )(labels, table)


def down(blocks):
    rows = NZ0 + 2 * PAD
    return pl.pallas_call(
        down_kernel,
        out_shape=[
            f32(6, 16, NZ0, LANES), f32(3, 16, NZ0, LANES), f32(3, 16, NZ0, LANES),
            f32(3, 16, NZ0, LANES), f32(4, 8, OWN1, LANES), f32(2, 8, HALO1, LANES),
            f32(2, 8, HALO1, LANES), f32(3, 8, LANES),
        ],
        in_specs=[VM],
        out_specs=[VM] * 8,
        scratch_shapes=[
            scratch(18, rows, LANES), scratch(17, rows, LANES), scratch(16, rows, LANES),
            scratch(16, rows, LANES), scratch(16, NZ0, LANES), scratch(3, 16, NZ0, LANES),
            scratch(3, 18, rows, LANES), scratch(3, 18, rows, LANES),
        ],
        compiler_params=params(),
        name="down",
    )(blocks)


def up(place, c0, v00, v01, g, own, below, above, diag):
    rows = NZ0 + 2 * PAD
    return pl.pallas_call(
        up_kernel,
        out_shape=[f32(3, LANES, LANES), f32(1, LANES)],
        in_specs=[SM] + [VM] * 8,
        out_specs=[VM] * 2,
        scratch_shapes=level_scratch(8, NZ1) + level_scratch(4, NZ2) + level_scratch(2, NZ3, True)
        + [
            scratch(3, 8, 144, LANES), scratch(3, 4, 80, LANES), scratch(3, 2, 80, LANES),
            scratch(3, 18, rows, LANES), scratch(3, 18, rows, LANES), scratch(9, 8, LANES),
        ],
        compiler_params=params(),
        name="up",
    )(place, c0, v00, v01, g, own, below, above, diag)


def from_below(x):
    n = lax.axis_size("dep")
    return lax.ppermute(x, "dep", [(i, i + 1) for i in range(n - 1)])


def from_above(x):
    n = lax.axis_size("dep")
    return lax.ppermute(x, "dep", [(i + 1, i) for i in range(n - 1)])


def body(labels, conductivity):
    k = conductivities(labels, conductivity)
    lower = from_below(k[OWN0 - HALO0 :])
    upper = from_above(k[:HALO0])
    column = jnp.concatenate([lower, k, upper], axis=0)
    plane = lax.axis_size("row") * lax.axis_size("col")
    blocks = lax.all_to_all(
        jnp.broadcast_to(column[None], (plane,) + column.shape), ("row", "col"), 0, 0
    )
    c0, v00, v01, g, own, low, high, diag = down(blocks)
    below = from_below(high)
    above = from_above(low)
    place = jnp.stack([lax.axis_index("row"), lax.axis_index("col")]).astype(jnp.int32)
    p, sums = up(place, c0, v00, v01, g, own, below, above, diag)
    depth = lax.axis_size("dep")
    parts = lax.all_to_all(jnp.broadcast_to(sums[None], (depth, 1, LANES)), "dep", 0, 0)
    cells = plane * labels.size * depth
    tensor = jnp.sum(parts, axis=(0, 1))[:9].reshape(3, 3) / cells
    return p.reshape((3,) + labels.shape), tensor


def solution(mesh):
    in_specs = (P("row", "col", "dep"), P())
    out_specs = (P(None, "row", "col", "dep"), P())
    return jax.shard_map(body, mesh=mesh, in_specs=in_specs, out_specs=out_specs, check_vma=False)
```

```python
import jax
import jax.numpy as jnp
from jax import lax
from jax.experimental import pallas as pl
from jax.experimental.pallas import tpu as pltpu
from jax.sharding import PartitionSpec as P


RELAX = 0.8
LANES = 128
PAD = 8
HALO0 = 4
HALO1 = 40
OWN0 = 128
OWN1 = 64
NZ0 = OWN0 + 2 * HALO0
NZ1 = OWN1 + 2 * HALO1
NZ2 = NZ1 // 2
NZ3 = 40
VMEM_LIMIT = 56 * 1024 * 1024


def lanes_of(shape=(8, LANES)):
    return lax.broadcasted_iota(jnp.int32, shape, 1)


def turned(tile, amount):
    return pltpu.roll(tile, amount % LANES, 1)


def span(start):
    return pl.ds(start, 8)


def strided(start):
    return pl.ds(start, 8, stride=2)


def harmonic(a, b):
    return (2.0 * a) * b * pl.reciprocal(jnp.maximum(a + b, 1e-30))


def over(lo, hi, step, carry=0):
    if hi - lo <= 80:
        for t in range(lo, hi, 8):
            carry = step(t, carry)
        return carry
    return lax.fori_loop(
        0, (hi - lo) // 8, lambda i, held: step(pl.multiple_of(lo + 8 * i, 8), held), carry
    )


def zero_pads(ref, lead, nz):
    zero = jnp.zeros((8, LANES), jnp.float32)
    for idx in lead:
        ref[(*idx, span(0), slice(None))] = zero
        ref[(*idx, span(PAD + nz), slice(None))] = zero


def cells_of(side):
    return [(x, y) for x in range(side) for y in range(side)]


def fields_of(side):
    return [(f, x, y) for f in range(3) for x, y in cells_of(side)]


def strides_of(level):
    return (32, 2) if level == 3 else (16, 1)


class Edges:
    def __init__(self, level):
        xs, ys = strides_of(level)
        lane = lanes_of()
        self.x_first, self.x_last = lane < xs, lane >= LANES - xs
        self.y_first, self.y_last = (lane & 15) < ys, (lane & 15) >= 16 - ys


def beside(read, side, level, x, y):
    xs, ys = strides_of(level)
    last = side - 1
    return [
        read(x + 1, y) if x < last else turned(read(0, y), -xs),
        read(x - 1, y) if x > 0 else turned(read(last, y), xs),
        read(x, y + 1) if y < last else turned(read(x, 0), -ys),
        read(x, y - 1) if y > 0 else turned(read(x, last), ys),
    ]


def coefficients(k, wx, wy, wz, emit, level, side, nz, carry=0):
    xs, ys = strides_of(level)
    last = side - 1
    edges = Edges(level)
    zero = jnp.zeros((8, LANES), jnp.float32)
    for x, y in cells_of(side):
        wz[x, y, span(0), :] = zero

    def faces(t, held):
        rows = span(PAD + t)
        for x, y in cells_of(side):
            kc = k[x, y, rows, :]
            if x < last:
                kx = k[x + 1, y, rows, :]
            else:
                kx = jnp.where(edges.x_last, 0.0, turned(k[0, y, rows, :], -xs))
            if y < last:
                ky = k[x, y + 1, rows, :]
            else:
                ky = jnp.where(edges.y_last, 0.0, turned(k[x, 0, rows, :], -ys))
            wx[x, y, rows, :] = harmonic(kc, kx)
            wy[x, y, rows, :] = harmonic(kc, ky)
            wz[x, y, rows, :] = harmonic(kc, k[x, y, span(PAD + t + 1), :])
        return held

    over(0, nz, faces)

    def cells(t, held):
        rows = span(PAD + t)
        for x, y in cells_of(side):
            kc = k[x, y, rows, :]
            weights = [
                wx[x, y, rows, :],
                wx[x - 1, y, rows, :] if x > 0 else turned(wx[last, y, rows, :], xs),
                wy[x, y, rows, :],
                wy[x, y - 1, rows, :] if y > 0 else turned(wy[x, last, rows, :], ys),
                wz[x, y, rows, :],
                wz[x, y, span(PAD + t - 1), :],
            ]
            outer = [
                edges.x_last if x == last else None,
                edges.x_first if x == 0 else None,
                edges.y_last if y == last else None,
                edges.y_first if y == 0 else None,
                k[x, y, span(PAD + t + 1), :] == 0.0,
                k[x, y, span(PAD + t - 1), :] == 0.0,
            ]
            full = [w if o is None else jnp.where(o, kc, w) for o, w in zip(outer, weights)]
            total = full[0]
            for w in full[1:]:
                total = total + w
            total = jnp.where(kc > 0.0, total, 1.0)
            held = emit(t, held, x, y, outer, weights, full, total)
        return held

    return over(0, nz, cells, carry)


def neighbours(c, v, side, level, x, y, t):
    coef = [c[n, x, y, span(t), :] for n in range(6)]
    centres, sums = [], []
    for f in range(3):
        near = beside(lambda i, j: v[f, i, j, span(PAD + t), :], side, level, x, y)
        near += [v[f, x, y, span(PAD + t + 1), :], v[f, x, y, span(PAD + t - 1), :]]
        parts = [a * b for a, b in zip(coef, near)]
        centres.append(v[f, x, y, span(PAD + t), :])
        sums.append(((parts[0] + parts[1]) + (parts[2] + parts[3])) + (parts[4] + parts[5]))
    return centres, sums


def sweep(c, v, first, out, level, side, lo, hi):
    def step(t, held):
        for x, y in cells_of(side):
            centres, sums = neighbours(c, v, side, level, x, y, t)
            for f in range(3):
                out[f, x, y, span(PAD + t), :] = sums[f] + (
                    first[f, x, y, span(t), :] + (1.0 - RELAX) * centres[f]
                )
        return held

    over(lo, hi, step)


def residual(c, v, first, invq, r, level, side, nz):
    def step(t, held):
        for x, y in cells_of(side):
            centres, sums = neighbours(c, v, side, level, x, y, t)
            scale = invq[x, y, span(t), :]
            for f in range(3):
                r[f, x, y, span(t), :] = (
                    sums[f] + (first[f, x, y, span(t), :] - RELAX * centres[f])
                ) * scale
        return held

    over(0, nz, step)


def mean8(read, x, y):
    total = None
    for dx in range(2):
        for dy in range(2):
            part = read(2 * x + dx, 2 * y + dy, 0) + read(2 * x + dx, 2 * y + dy, 1)
            total = part if total is None else total + part
    return total * 0.125


def mean8_lanes(read):
    lane = lanes_of()
    total = read(0, 0, 0) + read(0, 0, 1)
    for stride in (16, 1):
        mate = jnp.where((lane & stride) != 0, turned(total, stride), turned(total, -stride))
        total = total + mate
    return total * 0.125


def look_up(labels_ref, table_ref, out_ref, high_ref, low_ref, mixed):
    for x in range(8):
        for ylo in range(4):
            labels = labels_ref[x, pl.ds(ylo, 4, stride=4), :]
            k = jnp.zeros(labels.shape, jnp.float32)
            for phase in range(8):
                k = jnp.where(labels == phase, table_ref[phase], k)
            mixed[pl.ds((x % 4) * 32 + (x // 4) * 16 + ylo * 4, 4), :] = k
    column = mixed[...].T
    out_ref[...] = column
    low_ref[...] = column[:HALO0]
    high_ref[...] = column[OWN0 - HALO0 :]


def down_kernel(
    blocks, c_out, v0_out, v1_out, g_out, own, diag, k, wx, wy, wz, c, v0, g, invq, r, va, vb, sems
):
    lane = lanes_of()
    zero_pads(k, cells_of(4), NZ0)
    zero_pads(va, fields_of(4), NZ0)
    zero_pads(vb, fields_of(4), NZ0)

    def place(t, held):
        tiles = [blocks[n, span(t), :] for n in range(16)]
        for bit, stride in ((0, 4), (1, 8), (2, 32), (3, 64)):
            dist = 1 << bit
            clear = (lane & stride) == 0
            for i in range(16):
                if not i & dist:
                    a, b = tiles[i], tiles[i + dist]
                    tiles[i] = jnp.where(clear, a, turned(b, stride))
                    tiles[i + dist] = jnp.where(clear, turned(a, -stride), b)
        for x, y in cells_of(4):
            k[x, y, span(PAD + t), :] = tiles[4 * x + y]
        return held

    over(0, NZ0, place)

    def emit(t, held, x, y, outer, weights, full, total):
        rows = span(t)
        q = RELAX * pl.reciprocal(total)
        for n in range(6):
            c[n, x, y, rows, :] = q * weights[n]
        invq[x, y, rows, :] = (1.0 / RELAX) * total
        depth = lax.broadcasted_iota(jnp.int32, (8, LANES), 0) + (t - HALO0)
        inside = (depth >= 0) & (depth < OWN0)
        held = list(held)
        for f in range(3):
            up, down = full[2 * f], full[2 * f + 1]
            first = q * (down - up)
            v0[f, x, y, rows, :] = first
            va[f, x, y, span(PAD + t), :] = first
            upper, lower = outer[2 * f], outer[2 * f + 1]
            half_up = up if upper is None else jnp.where(upper, 0.5 * up, up)
            half_down = down if lower is None else jnp.where(lower, 0.5 * down, down)
            g[f, x, y, rows, :] = half_down - half_up
            held[f] = held[f] + jnp.where(inside, up + down, 0.0)
        return tuple(held)

    nothing = jnp.zeros((8, LANES), jnp.float32)
    sides = coefficients(k, wx, wy, wz, emit, 0, 4, NZ0, (nothing,) * 3)
    for f in range(3):
        diag[f, :, :] = 0.5 * sides[f]
    copies = [
        pltpu.make_async_copy(here, there, sems.at[n])
        for n, (here, there) in enumerate(((c, c_out), (v0, v0_out), (g, g_out), (vb, v1_out)))
    ]
    for copy in copies[:3]:
        copy.start()
    sweep(c, va, v0, vb, 0, 4, 0, NZ0)
    copies[3].start()
    residual(c, vb, v0, invq, r, 0, 4, NZ0)

    def coarse(t, held):
        for x, y in cells_of(2):
            for f in range(3):
                own[f, x, y, span(t), :] = mean8(
                    lambda i, j, dz: r[f, i, j, strided(HALO0 + 2 * t + dz), :], x, y
                )
            own[3, x, y, span(t), :] = mean8(
                lambda i, j, dz: k[i, j, strided(PAD + HALO0 + 2 * t + dz), :], x, y
            )
        return held

    over(0, OWN1, coarse)
    for copy in copies:
        copy.wait()


def up_kernel(
    c_in, v0_in, v1_in, g_in, own, below, above, diag,
    p, sums,
    k1, wx1, wy1, wz1, c1, f1, q1, r1, va1, vb1,
    k2, wx2, wy2, wz2, c2, f2, q2, r2, va2, vb2,
    k3, wx3, wy3, wz3, c3, f3, va3, vb3,
    wide1, wide2, wide3, va0, vb0, c0, v00, g, mixed, sems,
):
    lane = lanes_of()
    copies = [
        pltpu.make_async_copy(there, here, sems.at[n])
        for n, (here, there) in enumerate(((va0, v1_in), (c0, c_in), (v00, v0_in), (g, g_in)))
    ]
    for copy in copies:
        copy.start()

    for ref, base, count in ((below, 0, HALO1), (own, HALO1, OWN1), (above, HALO1 + OWN1, HALO1)):

        def fill(t, held):
            for x, y in cells_of(2):
                for f in range(3):
                    f1[f, x, y, span(base + t), :] = ref[f, x, y, span(t), :]
                k1[x, y, span(PAD + base + t), :] = ref[3, x, y, span(t), :]
            return held

        over(0, count, fill)

    def prepare(level, side, nz, k, wx, wy, wz, c, first, invq, va, vb):
        zero_pads(k, cells_of(side), nz)
        zero_pads(va, fields_of(side), nz)
        zero_pads(vb, fields_of(side), nz)
        scale = 4.0**level

        def emit(t, held, x, y, outer, weights, full, total):
            rows = span(t)
            q = RELAX * pl.reciprocal(total)
            for n in range(6):
                c[n, x, y, rows, :] = q * weights[n]
            if invq is not None:
                invq[x, y, rows, :] = (1.0 / (RELAX * scale)) * total
            for f in range(3):
                start = (q * scale) * first[f, x, y, rows, :]
                first[f, x, y, rows, :] = start
                va[f, x, y, span(PAD + t), :] = start
            return held

        coefficients(k, wx, wy, wz, emit, level, side, nz)

    def restrict(mean, side, nz, r, k, first, knext):
        def step(t, held):
            for x, y in cells_of(side):
                for f in range(3):
                    first[f, x, y, span(t), :] = mean(
                        lambda i, j, dz: r[f, i, j, strided(2 * t + dz), :], x, y
                    )
                knext[x, y, span(PAD + t), :] = mean(
                    lambda i, j, dz: k[i, j, strided(PAD + 2 * t + dz), :], x, y
                )
            return held

        over(0, nz, step)

    def widen(e, wide, side, first_row, count):
        def step(t, held):
            for f, x, y in fields_of(side):
                part = e[f, x, y, span(PAD + first_row + t), :]
                wide[f, x, y, strided(2 * t), :] = part
                wide[f, x, y, strided(2 * t + 1), :] = part
            return held

        over(0, count, step)

    def add_coarse(v, wide, side, ratio, lo, hi, first_row):
        def step(t, held):
            for f, x, y in fields_of(side):
                rows = span(PAD + t)
                v[f, x, y, rows, :] = (
                    v[f, x, y, rows, :] + wide[f, x // ratio, y // ratio, span(t - first_row), :]
                )
            return held

        over(lo, hi, step)

    prepare(1, 2, NZ1, k1, wx1, wy1, wz1, c1, f1, q1, va1, vb1)
    sweep(c1, va1, f1, vb1, 1, 2, 0, NZ1)
    residual(c1, vb1, f1, q1, r1, 1, 2, NZ1)
    restrict(mean8, 1, NZ2, r1, k1, f2, k2)

    prepare(2, 1, NZ2, k2, wx2, wy2, wz2, c2, f2, q2, va2, vb2)
    sweep(c2, va2, f2, vb2, 2, 1, 0, NZ2)
    for f in range(3):
        r2[f, 0, 0, span(NZ2), :] = jnp.zeros((8, LANES), jnp.float32)
    residual(c2, vb2, f2, q2, r2, 2, 1, NZ2)
    restrict(lambda read, x, y: mean8_lanes(read), 1, NZ3, r2, k2, f3, k3)

    prepare(3, 1, NZ3, k3, wx3, wy3, wz3, c3, f3, None, va3, vb3)
    sweep(c3, va3, f3, vb3, 3, 1, 0, NZ3)
    sweep(c3, vb3, f3, va3, 3, 1, 0, NZ3)
    sweep(c3, va3, f3, vb3, 3, 1, 0, NZ3)
    sweep(c3, vb3, f3, va3, 3, 1, 0, NZ3)
    sweep(c3, va3, f3, vb3, 3, 1, 0, NZ3)

    widen(vb3, wide3, 1, 0, NZ3)
    add_coarse(vb2, wide3, 1, 1, 0, NZ2, 0)
    sweep(c2, vb2, f2, va2, 2, 1, 0, NZ2)
    sweep(c2, va2, f2, vb2, 2, 1, 0, NZ2)

    lo1, hi1 = HALO1 - 8, HALO1 + OWN1 + 8
    widen(vb2, wide2, 1, lo1 // 2, (hi1 - lo1) // 2)
    add_coarse(vb1, wide2, 2, 2, lo1, hi1, lo1)
    sweep(c1, vb1, f1, va1, 1, 2, lo1, hi1)
    sweep(c1, va1, f1, vb1, 1, 2, lo1, hi1)

    widen(vb1, wide1, 2, HALO1 - HALO0 // 2, 72)
    zero_pads(vb0, fields_of(4), NZ0)
    for copy in copies:
        copy.wait()
    add_coarse(va0, wide1, 4, 2, 0, NZ0, 0)
    sweep(c0, va0, v00, vb0, 0, 4, 0, NZ0)

    def last(t, held):
        held = list(held)
        rows = span(HALO0 + t)
        for x, y in cells_of(4):
            centres, near = neighbours(c0, vb0, 4, 0, x, y, HALO0 + t)
            done = [
                near[f] + (v00[f, x, y, rows, :] + (1.0 - RELAX) * centres[f]) for f in range(3)
            ]
            for f in range(3):
                va0[f, x, y, span(t), :] = done[f]
            for i in range(3):
                gi = g[i, x, y, rows, :]
                for j in range(3):
                    held[3 * i + j] = held[3 * i + j] + gi * done[j]
        return tuple(held)

    nothing = jnp.zeros((8, LANES), jnp.float32)
    fluxes = over(0, OWN0, last, (nothing,) * 9)

    flat = jnp.zeros((1, LANES), jnp.float32)
    one_row = lax.broadcasted_iota(jnp.int32, (1, LANES), 1)
    for i in range(3):
        for j in range(3):
            part = fluxes[3 * i + j]
            if i == j:
                part = part + diag[i, :, :]
            whole = jnp.sum(jnp.sum(part, axis=0, keepdims=True), axis=1, keepdims=True)
            flat = jnp.where(one_row == 3 * i + j, whole, flat)
    sums[...] = flat

    start = lax.axis_index("row") * 32 + lax.axis_index("col") * 4
    for f in range(3):

        def gather(t, held):
            block = nothing
            for x, y in cells_of(4):
                amount = (32 * x + 4 * y + LANES - start) & (LANES - 1)
                piece = pltpu.roll(va0[f, x, y, span(t), :], amount, 1)
                block = jnp.where((lane & 0b1101100) == 32 * x + 4 * y, piece, block)
            mixed[span(t), :] = block
            return held

        over(0, OWN0, gather)
        block = mixed[...].T
        for x in range(8):
            for ylo in range(4):
                begin = (x % 4) * 32 + (x // 4) * 16 + ylo * 4
                p[f, x, pl.ds(ylo, 4, stride=4), :] = block[begin : begin + 4]


def f32(*shape):
    return jax.ShapeDtypeStruct(shape, jnp.float32)


def scratch(*shape):
    return pltpu.VMEM(shape, jnp.float32)


def level_scratch(side, nz, last=False):
    rows = nz + 2 * PAD
    got = [scratch(side, side, rows, LANES)] * 4
    got += [scratch(6, side, side, nz, LANES), scratch(3, side, side, nz, LANES)]
    if not last:
        got += [scratch(side, side, nz, LANES), scratch(3, side, side, nz + 8, LANES)]
    return got + [scratch(3, side, side, rows, LANES)] * 2


def params():
    return pltpu.CompilerParams(vmem_limit_bytes=VMEM_LIMIT)


VM = pl.BlockSpec(memory_space=pltpu.VMEM)
SM = pl.BlockSpec(memory_space=pltpu.SMEM)
HB = pl.BlockSpec(memory_space=pl.ANY)
ROWS0 = NZ0 + 2 * PAD


def conductivities(labels, table):
    return pl.pallas_call(
        look_up,
        out_shape=[f32(LANES, LANES), f32(HALO0, LANES), f32(HALO0, LANES)],
        in_specs=[VM, SM],
        out_specs=[VM] * 3,
        scratch_shapes=[scratch(LANES, LANES)],
        name="look_up",
    )(labels, table)


def down(blocks):
    return pl.pallas_call(
        down_kernel,
        out_shape=[
            f32(6, 4, 4, NZ0, LANES), f32(3, 4, 4, NZ0, LANES), f32(3, 4, 4, ROWS0, LANES),
            f32(3, 4, 4, NZ0, LANES), f32(4, 2, 2, OWN1, LANES), f32(3, 8, LANES),
        ],
        in_specs=[VM],
        out_specs=[HB] * 4 + [VM] * 2,
        scratch_shapes=[scratch(4, 4, ROWS0, LANES)] * 4
        + [
            scratch(6, 4, 4, NZ0, LANES), scratch(3, 4, 4, NZ0, LANES), scratch(3, 4, 4, NZ0, LANES),
            scratch(4, 4, NZ0, LANES), scratch(3, 4, 4, NZ0, LANES),
            scratch(3, 4, 4, ROWS0, LANES), scratch(3, 4, 4, ROWS0, LANES),
            pltpu.SemaphoreType.DMA((4,)),
        ],
        compiler_params=params(),
        name="down",
    )(blocks)


def up(c0, v00, v01, g, own, below, above, diag):
    return pl.pallas_call(
        up_kernel,
        out_shape=[f32(3, 8, 16, LANES), f32(1, LANES)],
        in_specs=[HB] * 4 + [VM] * 4,
        out_specs=[VM] * 2,
        scratch_shapes=level_scratch(2, NZ1) + level_scratch(1, NZ2) + level_scratch(1, NZ3, True)
        + [
            scratch(3, 2, 2, 144, LANES), scratch(3, 1, 1, 80, LANES), scratch(3, 1, 1, 80, LANES),
            scratch(3, 4, 4, ROWS0, LANES), scratch(3, 4, 4, ROWS0, LANES),
            scratch(6, 4, 4, NZ0, LANES), scratch(3, 4, 4, NZ0, LANES), scratch(3, 4, 4, NZ0, LANES),
            scratch(LANES, LANES), pltpu.SemaphoreType.DMA((4,)),
        ],
        compiler_params=params(),
        name="up",
    )(c0, v00, v01, g, own, below, above, diag)


def from_below(x):
    n = lax.axis_size("dep")
    return lax.ppermute(x, "dep", [(i, i + 1) for i in range(n - 1)])


def from_above(x):
    n = lax.axis_size("dep")
    return lax.ppermute(x, "dep", [(i + 1, i) for i in range(n - 1)])


def body(labels, conductivity):
    k, high, low = conductivities(labels, conductivity)
    column = jnp.concatenate([from_below(high), k, from_above(low)], axis=0)
    plane = lax.axis_size("row") * lax.axis_size("col")
    blocks = lax.all_to_all(
        jnp.broadcast_to(column[None], (plane,) + column.shape), ("row", "col"), 0, 0
    )
    c0, v00, v01, g, own, diag = down(blocks)
    below = from_below(own[:, :, :, OWN1 - HALO1 :])
    above = from_above(own[:, :, :, :HALO1])
    p, sums = up(c0, v00, v01, g, own, below, above, diag)
    depth = lax.axis_size("dep")
    parts = lax.all_to_all(jnp.broadcast_to(sums[None], (depth, 1, LANES)), "dep", 0, 0)
    cells = plane * labels.size * depth
    tensor = jnp.sum(parts, axis=(0, 1))[:9].reshape(3, 3) / cells
    return p, tensor


def solution(mesh):
    in_specs = (P("row", "col", "dep"), P())
    out_specs = (P(None, "row", "col", "dep"), P())
    return jax.shard_map(body, mesh=mesh, in_specs=in_specs, out_specs=out_specs, check_vma=False)
```

```python
import functools

import jax
import jax.numpy as jnp
from jax import lax
from jax.experimental import pallas as pl
from jax.experimental.pallas import tpu as pltpu
from jax.sharding import PartitionSpec as P


RELAX = 0.8
LANES = 128
PAD = 8
HALO0 = 4
HALO1 = 40
OWN0 = 128
OWN1 = 64
NZ0 = OWN0 + 2 * HALO0
NZ1 = OWN1 + 2 * HALO1
NZ2 = NZ1 // 2
NZ3 = 40
GROUPS = {4: 4, 2: 9, 1: 18}
VMEM_LIMIT = 34 * 1024 * 1024


def lanes_of(shape=(8, LANES)):
    return lax.broadcasted_iota(jnp.int32, shape, 1)


def turned(tile, amount):
    return pltpu.roll(tile, amount % LANES, 1)


def span(start):
    return pl.ds(start, 8)


def strided(start):
    return pl.ds(start, 8, stride=2)


def harmonic(a, b):
    return (2.0 * a) * b * pl.reciprocal(jnp.maximum(a + b, 1e-30))


def over(side, lo, hi, step, carry=0):
    group = GROUPS[side]
    whole = (hi - lo) // (8 * group)
    if whole <= 1:
        whole = 0

    def some(i, held):
        first = pl.multiple_of(lo + 8 * group * i, 8)
        for n in range(group):
            held = step(first + 8 * n, held)
        return held

    if whole:
        carry = lax.fori_loop(0, whole, some, carry)
    for t in range(lo + 8 * group * whole, hi, 8):
        carry = step(t, carry)
    return carry


def zero_pads(ref, lead, nz):
    zero = jnp.zeros((8, LANES), jnp.float32)
    for idx in lead:
        ref[(*idx, span(0), slice(None))] = zero
        ref[(*idx, span(PAD + nz), slice(None))] = zero


def cells_of(side):
    return [(x, y) for x in range(side) for y in range(side)]


def fields_of(side):
    return [(f, x, y) for f in range(3) for x, y in cells_of(side)]


def strides_of(level):
    return (32, 2) if level == 3 else (16, 1)


class Edges:
    def __init__(self, level):
        xs, ys = strides_of(level)
        lane = lanes_of()
        self.x_first, self.x_last = lane < xs, lane >= LANES - xs
        self.y_first, self.y_last = (lane & 15) < ys, (lane & 15) >= 16 - ys


def beside(read, side, level, x, y):
    xs, ys = strides_of(level)
    last = side - 1
    return [
        read(x + 1, y) if x < last else turned(read(0, y), -xs),
        read(x - 1, y) if x > 0 else turned(read(last, y), xs),
        read(x, y + 1) if y < last else turned(read(x, 0), -ys),
        read(x, y - 1) if y > 0 else turned(read(x, last), ys),
    ]


def coefficients(k, wx, wy, wz, emit, level, side, nz, carry=0):
    xs, ys = strides_of(level)
    last = side - 1
    edges = Edges(level)
    zero = jnp.zeros((8, LANES), jnp.float32)
    for x, y in cells_of(side):
        wz[x, y, span(0), :] = zero

    def faces(t, held):
        rows = span(PAD + t)
        for x, y in cells_of(side):
            kc = k[x, y, rows, :]
            if x < last:
                kx = k[x + 1, y, rows, :]
            else:
                kx = jnp.where(edges.x_last, 0.0, turned(k[0, y, rows, :], -xs))
            if y < last:
                ky = k[x, y + 1, rows, :]
            else:
                ky = jnp.where(edges.y_last, 0.0, turned(k[x, 0, rows, :], -ys))
            wx[x, y, rows, :] = harmonic(kc, kx)
            wy[x, y, rows, :] = harmonic(kc, ky)
            wz[x, y, rows, :] = harmonic(kc, k[x, y, span(PAD + t + 1), :])
        return held

    over(side, 0, nz, faces)

    def cells(t, held):
        rows = span(PAD + t)
        for x, y in cells_of(side):
            kc = k[x, y, rows, :]
            weights = [
                wx[x, y, rows, :],
                wx[x - 1, y, rows, :] if x > 0 else turned(wx[last, y, rows, :], xs),
                wy[x, y, rows, :],
                wy[x, y - 1, rows, :] if y > 0 else turned(wy[x, last, rows, :], ys),
                wz[x, y, rows, :],
                wz[x, y, span(PAD + t - 1), :],
            ]
            outer = [
                edges.x_last if x == last else None,
                edges.x_first if x == 0 else None,
                edges.y_last if y == last else None,
                edges.y_first if y == 0 else None,
                k[x, y, span(PAD + t + 1), :] == 0.0,
                k[x, y, span(PAD + t - 1), :] == 0.0,
            ]
            full = [w if o is None else jnp.where(o, kc, w) for o, w in zip(outer, weights)]
            total = full[0]
            for w in full[1:]:
                total = total + w
            total = jnp.where(kc > 0.0, total, 1.0)
            held = emit(t, held, x, y, outer, weights, full, total)
        return held

    return over(side, 0, nz, cells, carry)


def neighbours(c, v, side, level, x, y, t):
    coef = [c[n, x, y, span(t), :] for n in range(6)]
    centres, sums = [], []
    for f in range(3):
        near = beside(lambda i, j: v[f, i, j, span(PAD + t), :], side, level, x, y)
        near += [v[f, x, y, span(PAD + t + 1), :], v[f, x, y, span(PAD + t - 1), :]]
        parts = [a * b for a, b in zip(coef, near)]
        centres.append(v[f, x, y, span(PAD + t), :])
        sums.append(((parts[0] + parts[1]) + (parts[2] + parts[3])) + (parts[4] + parts[5]))
    return centres, sums


def sweep(c, v, first, out, level, side, lo, hi):
    def step(t, held):
        for x, y in cells_of(side):
            centres, sums = neighbours(c, v, side, level, x, y, t)
            for f in range(3):
                out[f, x, y, span(PAD + t), :] = sums[f] + (
                    first[f, x, y, span(t), :] + (1.0 - RELAX) * centres[f]
                )
        return held

    over(side, lo, hi, step)


def residual(c, v, first, invq, r, level, side, nz):
    def step(t, held):
        for x, y in cells_of(side):
            centres, sums = neighbours(c, v, side, level, x, y, t)
            scale = invq[x, y, span(t), :]
            for f in range(3):
                r[f, x, y, span(t), :] = (
                    sums[f] + (first[f, x, y, span(t), :] - RELAX * centres[f])
                ) * scale
        return held

    over(side, 0, nz, step)


def mean8(read, x, y):
    total = None
    for dx in range(2):
        for dy in range(2):
            part = read(2 * x + dx, 2 * y + dy, 0) + read(2 * x + dx, 2 * y + dy, 1)
            total = part if total is None else total + part
    return total * 0.125


def mean8_lanes(read):
    lane = lanes_of()
    total = read(0, 0, 0) + read(0, 0, 1)
    for stride in (16, 1):
        mate = jnp.where((lane & stride) != 0, turned(total, stride), turned(total, -stride))
        total = total + mate
    return total * 0.125


def look_up(labels_ref, table_ref, out_ref, high_ref, low_ref, mixed):
    for x in range(8):
        for ylo in range(4):
            labels = labels_ref[x, pl.ds(ylo, 4, stride=4), :]
            k = jnp.zeros(labels.shape, jnp.float32)
            for phase in range(8):
                k = jnp.where(labels == phase, table_ref[phase], k)
            mixed[pl.ds((x % 4) * 32 + (x // 4) * 16 + ylo * 4, 4), :] = k
    column = mixed[...].T
    out_ref[...] = column
    low_ref[...] = column[:HALO0]
    high_ref[...] = column[OWN0 - HALO0 :]


def down_kernel(
    blocks, c_out, v0_out, v1_out, g_out, own, low, high, diag, k, wx, wy, wz, c, v0, g, invq, r, va, vb, sems
):
    lane = lanes_of()
    zero_pads(k, cells_of(4), NZ0)
    zero_pads(va, fields_of(4), NZ0)
    zero_pads(vb, fields_of(4), NZ0)

    def place(t, held):
        tiles = [blocks[n, span(t), :] for n in range(16)]
        for bit, stride in ((0, 4), (1, 8), (2, 32), (3, 64)):
            dist = 1 << bit
            clear = (lane & stride) == 0
            for i in range(16):
                if not i & dist:
                    a, b = tiles[i], tiles[i + dist]
                    tiles[i] = jnp.where(clear, a, turned(b, stride))
                    tiles[i + dist] = jnp.where(clear, turned(a, -stride), b)
        for x, y in cells_of(4):
            k[x, y, span(PAD + t), :] = tiles[4 * x + y]
        return held

    over(4, 0, NZ0, place)

    def emit(t, held, x, y, outer, weights, full, total):
        rows = span(t)
        q = RELAX * pl.reciprocal(total)
        for n in range(6):
            c[n, x, y, rows, :] = q * weights[n]
        invq[x, y, rows, :] = (1.0 / RELAX) * total
        depth = lax.broadcasted_iota(jnp.int32, (8, LANES), 0) + (t - HALO0)
        inside = (depth >= 0) & (depth < OWN0)
        held = list(held)
        for f in range(3):
            up, down = full[2 * f], full[2 * f + 1]
            first = q * (down - up)
            v0[f, x, y, rows, :] = first
            va[f, x, y, span(PAD + t), :] = first
            upper, lower = outer[2 * f], outer[2 * f + 1]
            half_up = up if upper is None else jnp.where(upper, 0.5 * up, up)
            half_down = down if lower is None else jnp.where(lower, 0.5 * down, down)
            g[f, x, y, rows, :] = half_down - half_up
            held[f] = held[f] + jnp.where(inside, up + down, 0.0)
        return tuple(held)

    nothing = jnp.zeros((8, LANES), jnp.float32)
    sides = coefficients(k, wx, wy, wz, emit, 0, 4, NZ0, (nothing,) * 3)
    for f in range(3):
        diag[f, :, :] = 0.5 * sides[f]
    copies = [
        pltpu.make_async_copy(here, there, sems.at[n])
        for n, (here, there) in enumerate(((c, c_out), (v0, v0_out), (g, g_out), (vb, v1_out)))
    ]
    for copy in copies[:3]:
        copy.start()
    sweep(c, va, v0, vb, 0, 4, 0, NZ0)
    copies[3].start()
    residual(c, vb, v0, invq, r, 0, 4, NZ0)

    def coarse(t, held):
        for x, y in cells_of(2):
            for f in range(3):
                own[f, x, y, span(t), :] = mean8(
                    lambda i, j, dz: r[f, i, j, strided(HALO0 + 2 * t + dz), :], x, y
                )
            own[3, x, y, span(t), :] = mean8(
                lambda i, j, dz: k[i, j, strided(PAD + HALO0 + 2 * t + dz), :], x, y
            )
        return held

    over(4, 0, OWN1, coarse)
    for n in range(4):
        for x, y in cells_of(2):
            low[n, x, y, :, :] = own[n, x, y, pl.ds(0, HALO1), :]
            high[n, x, y, :, :] = own[n, x, y, pl.ds(OWN1 - HALO1, HALO1), :]
    for copy in copies:
        copy.wait()


def up_kernel(
    share, c_in, v0_in, v1_in, g_in, own, below, above, diag,
    p, sums,
    k1, wx1, wy1, wz1, c1, f1, q1, r1, va1, vb1,
    k2, wx2, wy2, wz2, c2, f2, q2, r2, va2, vb2,
    k3, wx3, wy3, wz3, c3, f3, va3, vb3,
    wide1, wide2, wide3, va0, vb0, c0, v00, g, mixed, sems,
):
    lane = lanes_of()
    copies = [
        pltpu.make_async_copy(there, here, sems.at[n])
        for n, (here, there) in enumerate(((va0, v1_in), (c0, c_in), (v00, v0_in), (g, g_in)))
    ]
    for copy in copies:
        copy.start()

    for ref, base, count in ((below, 0, HALO1), (own, HALO1, OWN1), (above, HALO1 + OWN1, HALO1)):

        def fill(t, held):
            for x, y in cells_of(2):
                for f in range(3):
                    f1[f, x, y, span(base + t), :] = ref[f, x, y, span(t), :]
                k1[x, y, span(PAD + base + t), :] = ref[3, x, y, span(t), :]
            return held

        over(2, 0, count, fill)

    def prepare(level, side, nz, k, wx, wy, wz, c, first, invq, va, vb):
        zero_pads(k, cells_of(side), nz)
        zero_pads(va, fields_of(side), nz)
        zero_pads(vb, fields_of(side), nz)
        scale = 4.0**level

        def emit(t, held, x, y, outer, weights, full, total):
            rows = span(t)
            q = RELAX * pl.reciprocal(total)
            for n in range(6):
                c[n, x, y, rows, :] = q * weights[n]
            if invq is not None:
                invq[x, y, rows, :] = (1.0 / (RELAX * scale)) * total
            for f in range(3):
                start = (q * scale) * first[f, x, y, rows, :]
                first[f, x, y, rows, :] = start
                va[f, x, y, span(PAD + t), :] = start
            return held

        coefficients(k, wx, wy, wz, emit, level, side, nz)

    def restrict(mean, side, nz, r, k, first, knext):
        def step(t, held):
            for x, y in cells_of(side):
                for f in range(3):
                    first[f, x, y, span(t), :] = mean(
                        lambda i, j, dz: r[f, i, j, strided(2 * t + dz), :], x, y
                    )
                knext[x, y, span(PAD + t), :] = mean(
                    lambda i, j, dz: k[i, j, strided(PAD + 2 * t + dz), :], x, y
                )
            return held

        over(2 * side, 0, nz, step)

    def widen(e, wide, side, first_row, count):
        def step(t, held):
            for f, x, y in fields_of(side):
                part = e[f, x, y, span(PAD + first_row + t), :]
                wide[f, x, y, strided(2 * t), :] = part
                wide[f, x, y, strided(2 * t + 1), :] = part
            return held

        over(2 * side, 0, count, step)

    def add_coarse(v, wide, side, ratio, lo, hi, first_row):
        def step(t, held):
            for f, x, y in fields_of(side):
                rows = span(PAD + t)
                v[f, x, y, rows, :] = (
                    v[f, x, y, rows, :] + wide[f, x // ratio, y // ratio, span(t - first_row), :]
                )
            return held

        over(side, lo, hi, step)

    prepare(1, 2, NZ1, k1, wx1, wy1, wz1, c1, f1, q1, va1, vb1)
    sweep(c1, va1, f1, vb1, 1, 2, 0, NZ1)
    residual(c1, vb1, f1, q1, r1, 1, 2, NZ1)
    restrict(mean8, 1, NZ2, r1, k1, f2, k2)

    prepare(2, 1, NZ2, k2, wx2, wy2, wz2, c2, f2, q2, va2, vb2)
    sweep(c2, va2, f2, vb2, 2, 1, 0, NZ2)
    for f in range(3):
        r2[f, 0, 0, span(NZ2), :] = jnp.zeros((8, LANES), jnp.float32)
    residual(c2, vb2, f2, q2, r2, 2, 1, NZ2)
    restrict(lambda read, x, y: mean8_lanes(read), 1, NZ3, r2, k2, f3, k3)

    prepare(3, 1, NZ3, k3, wx3, wy3, wz3, c3, f3, None, va3, vb3)
    sweep(c3, va3, f3, vb3, 3, 1, 0, NZ3)
    sweep(c3, vb3, f3, va3, 3, 1, 0, NZ3)
    sweep(c3, va3, f3, vb3, 3, 1, 0, NZ3)
    sweep(c3, vb3, f3, va3, 3, 1, 0, NZ3)
    sweep(c3, va3, f3, vb3, 3, 1, 0, NZ3)

    widen(vb3, wide3, 1, 0, NZ3)
    add_coarse(vb2, wide3, 1, 1, 0, NZ2, 0)
    sweep(c2, vb2, f2, va2, 2, 1, 0, NZ2)
    sweep(c2, va2, f2, vb2, 2, 1, 0, NZ2)

    lo1, hi1 = HALO1 - 8, HALO1 + OWN1 + 8
    widen(vb2, wide2, 1, lo1 // 2, (hi1 - lo1) // 2)
    add_coarse(vb1, wide2, 2, 2, lo1, hi1, lo1)
    sweep(c1, vb1, f1, va1, 1, 2, lo1, hi1)
    sweep(c1, va1, f1, vb1, 1, 2, lo1, hi1)

    widen(vb1, wide1, 2, HALO1 - HALO0 // 2, 72)
    zero_pads(vb0, fields_of(4), NZ0)
    for copy in copies:
        copy.wait()
    add_coarse(va0, wide1, 4, 2, 0, NZ0, 0)
    sweep(c0, va0, v00, vb0, 0, 4, 0, NZ0)

    def last(t, held):
        held = list(held)
        rows = span(HALO0 + t)
        for x, y in cells_of(4):
            centres, near = neighbours(c0, vb0, 4, 0, x, y, HALO0 + t)
            done = [
                near[f] + (v00[f, x, y, rows, :] + (1.0 - RELAX) * centres[f]) for f in range(3)
            ]
            for f in range(3):
                va0[f, x, y, span(t), :] = done[f]
            for i in range(3):
                gi = g[i, x, y, rows, :]
                for j in range(3):
                    held[3 * i + j] = held[3 * i + j] + gi * done[j]
        return tuple(held)

    nothing = jnp.zeros((8, LANES), jnp.float32)
    fluxes = over(4, 0, OWN0, last, (nothing,) * 9)

    flat = jnp.zeros((1, LANES), jnp.float32)
    one_row = lax.broadcasted_iota(jnp.int32, (1, LANES), 1)
    for i in range(3):
        for j in range(3):
            part = fluxes[3 * i + j]
            if i == j:
                part = part + diag[i, :, :]
            whole = jnp.sum(jnp.sum(part, axis=0, keepdims=True), axis=1, keepdims=True)
            flat = jnp.where(one_row == 3 * i + j, whole, flat)
    flat = flat * share
    for n in range(sums.shape[0]):
        sums[n, :, :] = flat

    start = lax.axis_index("row") * 32 + lax.axis_index("col") * 4
    for f in range(3):

        def gather(t, held):
            block = nothing
            for x, y in cells_of(4):
                amount = (32 * x + 4 * y + LANES - start) & (LANES - 1)
                piece = pltpu.roll(va0[f, x, y, span(t), :], amount, 1)
                block = jnp.where((lane & 0b1101100) == 32 * x + 4 * y, piece, block)
            mixed[span(t), :] = block
            return held

        over(4, 0, OWN0, gather)
        block = mixed[...].T
        for x in range(8):
            for ylo in range(4):
                begin = (x % 4) * 32 + (x // 4) * 16 + ylo * 4
                p[f, x, pl.ds(ylo, 4, stride=4), :] = block[begin : begin + 4]


def f32(*shape):
    return jax.ShapeDtypeStruct(shape, jnp.float32)


def scratch(*shape):
    return pltpu.VMEM(shape, jnp.float32)


def level_scratch(side, nz, last=False):
    rows = nz + 2 * PAD
    got = [scratch(side, side, rows, LANES)] * 4
    got += [scratch(6, side, side, nz, LANES), scratch(3, side, side, nz, LANES)]
    if not last:
        got += [scratch(side, side, nz, LANES), scratch(3, side, side, nz + 8, LANES)]
    return got + [scratch(3, side, side, rows, LANES)] * 2


def params():
    return pltpu.CompilerParams(vmem_limit_bytes=VMEM_LIMIT)


VM = pl.BlockSpec(memory_space=pltpu.VMEM)
SM = pl.BlockSpec(memory_space=pltpu.SMEM)
HB = pl.BlockSpec(memory_space=pl.ANY)
ROWS0 = NZ0 + 2 * PAD


def conductivities(labels, table):
    return pl.pallas_call(
        look_up,
        out_shape=[f32(LANES, LANES), f32(HALO0, LANES), f32(HALO0, LANES)],
        in_specs=[VM, SM],
        out_specs=[VM] * 3,
        scratch_shapes=[scratch(LANES, LANES)],
        name="look_up",
    )(labels, table)


def down(blocks):
    return pl.pallas_call(
        down_kernel,
        out_shape=[
            f32(6, 4, 4, NZ0, LANES), f32(3, 4, 4, NZ0, LANES), f32(3, 4, 4, ROWS0, LANES),
            f32(3, 4, 4, NZ0, LANES), f32(4, 2, 2, OWN1, LANES), f32(4, 2, 2, HALO1, LANES),
            f32(4, 2, 2, HALO1, LANES), f32(3, 8, LANES),
        ],
        in_specs=[VM],
        out_specs=[HB] * 4 + [VM] * 4,
        scratch_shapes=[scratch(4, 4, ROWS0, LANES)] * 4
        + [
            scratch(6, 4, 4, NZ0, LANES), scratch(3, 4, 4, NZ0, LANES), scratch(3, 4, 4, NZ0, LANES),
            scratch(4, 4, NZ0, LANES), scratch(3, 4, 4, NZ0, LANES),
            scratch(3, 4, 4, ROWS0, LANES), scratch(3, 4, 4, ROWS0, LANES),
            pltpu.SemaphoreType.DMA((4,)),
        ],
        compiler_params=params(),
        name="down",
    )(blocks)


def up(c0, v00, v01, g, own, below, above, diag, depth, cells):
    return pl.pallas_call(
        functools.partial(up_kernel, 1.0 / cells),
        out_shape=[f32(3, 8, 16, LANES), f32(depth, 1, LANES)],
        in_specs=[HB] * 4 + [VM] * 4,
        out_specs=[VM] * 2,
        scratch_shapes=level_scratch(2, NZ1) + level_scratch(1, NZ2) + level_scratch(1, NZ3, True)
        + [
            scratch(3, 2, 2, 144, LANES), scratch(3, 1, 1, 80, LANES), scratch(3, 1, 1, 80, LANES),
            scratch(3, 4, 4, ROWS0, LANES), scratch(3, 4, 4, ROWS0, LANES),
            scratch(6, 4, 4, NZ0, LANES), scratch(3, 4, 4, NZ0, LANES), scratch(3, 4, 4, NZ0, LANES),
            scratch(LANES, LANES), pltpu.SemaphoreType.DMA((4,)),
        ],
        compiler_params=params(),
        name="up",
    )(c0, v00, v01, g, own, below, above, diag)


def from_below(x):
    n = lax.axis_size("dep")
    return lax.ppermute(x, "dep", [(i, i + 1) for i in range(n - 1)])


def from_above(x):
    n = lax.axis_size("dep")
    return lax.ppermute(x, "dep", [(i + 1, i) for i in range(n - 1)])


def body(labels, conductivity):
    k, high, low = conductivities(labels, conductivity)
    column = jnp.concatenate([from_below(high), k, from_above(low)], axis=0)
    plane = lax.axis_size("row") * lax.axis_size("col")
    blocks = lax.all_to_all(
        jnp.broadcast_to(column[None], (plane,) + column.shape), ("row", "col"), 0, 0
    )
    c0, v00, v01, g, own, low, high, diag = down(blocks)
    above = from_above(low)
    below = from_below(high)
    depth = lax.axis_size("dep")
    cells = plane * labels.size * depth
    p, sums = up(c0, v00, v01, g, own, below, above, diag, depth, cells)
    parts = lax.all_to_all(sums, "dep", 0, 0)
    tensor = jnp.sum(parts, axis=(0, 1))[:9].reshape(3, 3)
    return p, tensor


def solution(mesh):
    in_specs = (P("row", "col", "dep"), P())
    out_specs = (P(None, "row", "col", "dep"), P())
    return jax.shard_map(body, mesh=mesh, in_specs=in_specs, out_specs=out_specs, check_vma=False)
```

```python
import functools

import jax
import jax.numpy as jnp
from jax import lax
from jax.experimental import pallas as pl
from jax.experimental.pallas import tpu as pltpu
from jax.sharding import PartitionSpec as P


RELAX = 0.8
LANES = 128
PAD = 8
HALO0 = 4
HALO1 = 40
OWN0 = 128
OWN1 = 64
NZ0 = OWN0 + 2 * HALO0
NZ1 = OWN1 + 2 * HALO1
NZ2 = NZ1 // 2
NZ3 = 40
GROUPS = {4: 4, 2: 9, 1: 18}
VMEM_LIMIT = 34 * 1024 * 1024


def lanes_of(shape=(8, LANES)):
    return lax.broadcasted_iota(jnp.int32, shape, 1)


def turned(tile, amount):
    return pltpu.roll(tile, amount % LANES, 1)


def span(start):
    return pl.ds(start, 8)


def strided(start):
    return pl.ds(start, 8, stride=2)


def harmonic(a, b):
    return (2.0 * a) * b * pl.reciprocal(jnp.maximum(a + b, 1e-30))


def over(side, lo, hi, step, carry=0):
    group = GROUPS[side]
    whole = (hi - lo) // (8 * group)
    if whole <= 1:
        whole = 0

    def some(i, held):
        first = pl.multiple_of(lo + 8 * group * i, 8)
        for n in range(group):
            held = step(first + 8 * n, held)
        return held

    if whole:
        carry = lax.fori_loop(0, whole, some, carry)
    for t in range(lo + 8 * group * whole, hi, 8):
        carry = step(t, carry)
    return carry


def zero_pads(ref, lead, nz):
    zero = jnp.zeros((8, LANES), jnp.float32)
    for idx in lead:
        ref[(*idx, span(0), slice(None))] = zero
        ref[(*idx, span(PAD + nz), slice(None))] = zero


def cells_of(side):
    return [(x, y) for x in range(side) for y in range(side)]


def fields_of(side):
    return [(f, x, y) for f in range(3) for x, y in cells_of(side)]


def strides_of(level):
    return (32, 2) if level == 3 else (16, 1)


class Edges:
    def __init__(self, level):
        xs, ys = strides_of(level)
        lane = lanes_of()
        self.x_first, self.x_last = lane < xs, lane >= LANES - xs
        self.y_first, self.y_last = (lane & 15) < ys, (lane & 15) >= 16 - ys


def beside(read, side, level, x, y):
    xs, ys = strides_of(level)
    last = side - 1
    return [
        read(x + 1, y) if x < last else turned(read(0, y), -xs),
        read(x - 1, y) if x > 0 else turned(read(last, y), xs),
        read(x, y + 1) if y < last else turned(read(x, 0), -ys),
        read(x, y - 1) if y > 0 else turned(read(x, last), ys),
    ]


def coefficients(k, wx, wy, wz, emit, level, side, nz, carry=0):
    xs, ys = strides_of(level)
    last = side - 1
    edges = Edges(level)
    zero = jnp.zeros((8, LANES), jnp.float32)
    for x, y in cells_of(side):
        wz[x, y, span(0), :] = zero

    def faces(t, held):
        rows = span(PAD + t)
        for x, y in cells_of(side):
            kc = k[x, y, rows, :]
            if x < last:
                kx = k[x + 1, y, rows, :]
            else:
                kx = jnp.where(edges.x_last, 0.0, turned(k[0, y, rows, :], -xs))
            if y < last:
                ky = k[x, y + 1, rows, :]
            else:
                ky = jnp.where(edges.y_last, 0.0, turned(k[x, 0, rows, :], -ys))
            wx[x, y, rows, :] = harmonic(kc, kx)
            wy[x, y, rows, :] = harmonic(kc, ky)
            wz[x, y, rows, :] = harmonic(kc, k[x, y, span(PAD + t + 1), :])
        return held

    over(side, 0, nz, faces)

    def cells(t, held):
        rows = span(PAD + t)
        for x, y in cells_of(side):
            kc = k[x, y, rows, :]
            weights = [
                wx[x, y, rows, :],
                wx[x - 1, y, rows, :] if x > 0 else turned(wx[last, y, rows, :], xs),
                wy[x, y, rows, :],
                wy[x, y - 1, rows, :] if y > 0 else turned(wy[x, last, rows, :], ys),
                wz[x, y, rows, :],
                wz[x, y, span(PAD + t - 1), :],
            ]
            outer = [
                edges.x_last if x == last else None,
                edges.x_first if x == 0 else None,
                edges.y_last if y == last else None,
                edges.y_first if y == 0 else None,
                weights[4] == 0.0,
                weights[5] == 0.0,
            ]
            full = [w if o is None else jnp.where(o, kc, w) for o, w in zip(outer, weights)]
            total = full[0]
            for w in full[1:]:
                total = total + w
            total = jnp.where(kc > 0.0, total, 1.0)
            held = emit(t, held, x, y, outer, weights, full, total)
        return held

    return over(side, 0, nz, cells, carry)


def neighbours(c, v, side, level, x, y, t):
    coef = [c[n, x, y, span(t), :] for n in range(6)]
    centres, sums = [], []
    for f in range(3):
        near = beside(lambda i, j: v[f, i, j, span(PAD + t), :], side, level, x, y)
        near += [v[f, x, y, span(PAD + t + 1), :], v[f, x, y, span(PAD + t - 1), :]]
        parts = [a * b for a, b in zip(coef, near)]
        centres.append(v[f, x, y, span(PAD + t), :])
        sums.append(((parts[0] + parts[1]) + (parts[2] + parts[3])) + (parts[4] + parts[5]))
    return centres, sums


def sweep(c, v, first, out, level, side, lo, hi, base=0):
    def step(t, held):
        for x, y in cells_of(side):
            centres, sums = neighbours(c, v, side, level, x, y, t)
            for f in range(3):
                out[f, x, y, span(PAD + t), :] = sums[f] + (
                    (2.0 - RELAX) * centres[f]
                    if first is v
                    else first[f, x, y, span(base + t), :] + (1.0 - RELAX) * centres[f]
                )
        return held

    over(side, lo, hi, step)


def residual(c, v, first, invq, r, level, side, nz, base=0):
    def step(t, held):
        for x, y in cells_of(side):
            centres, sums = neighbours(c, v, side, level, x, y, t)
            scale = invq[x, y, span(t), :]
            for f in range(3):
                r[f, x, y, span(t), :] = (
                    sums[f] + (first[f, x, y, span(base + t), :] - RELAX * centres[f])
                ) * scale
        return held

    over(side, 0, nz, step)


def mean8(read, x, y):
    total = None
    for dx in range(2):
        for dy in range(2):
            part = read(2 * x + dx, 2 * y + dy, 0) + read(2 * x + dx, 2 * y + dy, 1)
            total = part if total is None else total + part
    return total * 0.125


def mean8_lanes(read):
    lane = lanes_of()
    total = read(0, 0, 0) + read(0, 0, 1)
    for stride in (16, 1):
        mate = jnp.where((lane & stride) != 0, turned(total, stride), turned(total, -stride))
        total = total + mate
    return total * 0.125


def look_up(labels_ref, table_ref, out_ref, high_ref, low_ref, mixed):
    for x in range(8):
        for ylo in range(4):
            labels = labels_ref[x, pl.ds(ylo, 4, stride=4), :]
            k = jnp.zeros(labels.shape, jnp.float32)
            for phase in range(8):
                k = jnp.where(labels == phase, table_ref[phase], k)
            mixed[pl.ds((x % 4) * 32 + (x // 4) * 16 + ylo * 4, 4), :] = k
    column = mixed[...].T
    out_ref[...] = column
    low_ref[...] = column[:HALO0]
    high_ref[...] = column[OWN0 - HALO0 :]


def down_kernel(
    blocks, c_out, v0_out, v1_out, g_out, own, low, high, diag, k, wx, wy, wz, c, g, invq, r, va, vb, sems
):
    lane = lanes_of()
    zero_pads(k, cells_of(4), NZ0)
    zero_pads(va, fields_of(4), NZ0)
    zero_pads(vb, fields_of(4), NZ0)

    for t in range(0, NZ0, 8):
        tiles = [blocks[n, span(t), :] for n in range(16)]
        for bit, stride in ((0, 4), (1, 8), (2, 32), (3, 64)):
            dist = 1 << bit
            clear = (lane & stride) == 0
            for i in range(16):
                if not i & dist:
                    a, b = tiles[i], tiles[i + dist]
                    tiles[i] = jnp.where(clear, a, turned(b, stride))
                    tiles[i + dist] = jnp.where(clear, turned(a, -stride), b)
        for x, y in cells_of(4):
            k[x, y, span(PAD + t), :] = tiles[4 * x + y]

    def emit(t, held, x, y, outer, weights, full, total):
        rows = span(t)
        q = RELAX * pl.reciprocal(total)
        for n in range(6):
            c[n, x, y, rows, :] = q * weights[n]
        invq[x, y, rows, :] = (1.0 / RELAX) * total
        depth = lax.broadcasted_iota(jnp.int32, (8, LANES), 0) + (t - HALO0)
        inside = (depth >= 0) & (depth < OWN0)
        held = list(held)
        for f in range(3):
            up, down = full[2 * f], full[2 * f + 1]
            first = q * (down - up)
            va[f, x, y, span(PAD + t), :] = first
            upper, lower = outer[2 * f], outer[2 * f + 1]
            half_up = up if upper is None else jnp.where(upper, 0.5 * up, up)
            half_down = down if lower is None else jnp.where(lower, 0.5 * down, down)
            g[f, x, y, rows, :] = half_down - half_up
            held[f] = held[f] + jnp.where(inside, up + down, 0.0)
        return tuple(held)

    nothing = jnp.zeros((8, LANES), jnp.float32)
    sides = coefficients(k, wx, wy, wz, emit, 0, 4, NZ0, (nothing,) * 3)
    for f in range(3):
        diag[f, :, :] = 0.5 * sides[f]
    copies = [
        pltpu.make_async_copy(here, there, sems.at[n])
        for n, (here, there) in enumerate(((c, c_out), (va, v0_out), (g, g_out), (vb, v1_out)))
    ]
    for copy in copies[:3]:
        copy.start()
    sweep(c, va, va, vb, 0, 4, 0, NZ0)
    copies[3].start()
    residual(c, vb, va, invq, r, 0, 4, NZ0, PAD)

    def coarse(t, held):
        for x, y in cells_of(2):
            for f in range(3):
                own[f, x, y, span(t), :] = mean8(
                    lambda i, j, dz: r[f, i, j, strided(HALO0 + 2 * t + dz), :], x, y
                )
            own[3, x, y, span(t), :] = mean8(
                lambda i, j, dz: k[i, j, strided(PAD + HALO0 + 2 * t + dz), :], x, y
            )
        return held

    over(4, 0, OWN1, coarse)
    for n in range(4):
        for x, y in cells_of(2):
            low[n, x, y, :, :] = own[n, x, y, pl.ds(0, HALO1), :]
            high[n, x, y, :, :] = own[n, x, y, pl.ds(OWN1 - HALO1, HALO1), :]
    for copy in copies:
        copy.wait()


def up_kernel(
    share, c_in, v0_in, v1_in, g_in, own, below, above, diag,
    p, sums,
    k1, wx1, wy1, wz1, c1, f1, q1, r1, va1, vb1,
    k2, wx2, wy2, wz2, c2, f2, q2, r2, va2, vb2,
    k3, wx3, wy3, wz3, c3, f3, va3, vb3,
    wide1, wide2, wide3, va0, vb0, c0, v00, g, mixed, sems,
):
    lane = lanes_of()
    copies = [
        pltpu.make_async_copy(there, here, sems.at[n])
        for n, (here, there) in enumerate(((va0, v1_in), (c0, c_in), (v00, v0_in), (g, g_in)))
    ]
    for copy in copies:
        copy.start()

    for ref, base, count in ((below, 0, HALO1), (own, HALO1, OWN1), (above, HALO1 + OWN1, HALO1)):

        def fill(t, held):
            for x, y in cells_of(2):
                for f in range(3):
                    f1[f, x, y, span(base + t), :] = ref[f, x, y, span(t), :]
                k1[x, y, span(PAD + base + t), :] = ref[3, x, y, span(t), :]
            return held

        over(2, 0, count, fill)

    def prepare(level, side, nz, k, wx, wy, wz, c, first, invq, va, vb):
        zero_pads(k, cells_of(side), nz)
        zero_pads(va, fields_of(side), nz)
        zero_pads(vb, fields_of(side), nz)
        scale = 4.0**level

        def emit(t, held, x, y, outer, weights, full, total):
            rows = span(t)
            q = RELAX * pl.reciprocal(total)
            for n in range(6):
                c[n, x, y, rows, :] = q * weights[n]
            if invq is not None:
                invq[x, y, rows, :] = (1.0 / (RELAX * scale)) * total
            for f in range(3):
                start = (q * scale) * first[f, x, y, rows, :]
                first[f, x, y, rows, :] = start
                va[f, x, y, span(PAD + t), :] = start
            return held

        coefficients(k, wx, wy, wz, emit, level, side, nz)

    def restrict(mean, side, nz, r, k, first, knext):
        def step(t, held):
            for x, y in cells_of(side):
                for f in range(3):
                    first[f, x, y, span(t), :] = mean(
                        lambda i, j, dz: r[f, i, j, strided(2 * t + dz), :], x, y
                    )
                knext[x, y, span(PAD + t), :] = mean(
                    lambda i, j, dz: k[i, j, strided(PAD + 2 * t + dz), :], x, y
                )
            return held

        over(2 * side, 0, nz, step)

    def widen(e, wide, side, first_row, count):
        def step(t, held):
            for f, x, y in fields_of(side):
                part = e[f, x, y, span(PAD + first_row + t), :]
                wide[f, x, y, strided(2 * t), :] = part
                wide[f, x, y, strided(2 * t + 1), :] = part
            return held

        over(2 * side, 0, count, step)

    def add_coarse(v, wide, side, ratio, lo, hi, first_row):
        def step(t, held):
            for f, x, y in fields_of(side):
                rows = span(PAD + t)
                v[f, x, y, rows, :] = (
                    v[f, x, y, rows, :] + wide[f, x // ratio, y // ratio, span(t - first_row), :]
                )
            return held

        over(side, lo, hi, step)

    prepare(1, 2, NZ1, k1, wx1, wy1, wz1, c1, f1, q1, va1, vb1)
    sweep(c1, va1, f1, vb1, 1, 2, 0, NZ1)
    residual(c1, vb1, f1, q1, r1, 1, 2, NZ1)
    restrict(mean8, 1, NZ2, r1, k1, f2, k2)

    prepare(2, 1, NZ2, k2, wx2, wy2, wz2, c2, f2, q2, va2, vb2)
    sweep(c2, va2, f2, vb2, 2, 1, 0, NZ2)
    for f in range(3):
        r2[f, 0, 0, span(NZ2), :] = jnp.zeros((8, LANES), jnp.float32)
    residual(c2, vb2, f2, q2, r2, 2, 1, NZ2)
    restrict(lambda read, x, y: mean8_lanes(read), 1, NZ3, r2, k2, f3, k3)

    prepare(3, 1, NZ3, k3, wx3, wy3, wz3, c3, f3, None, va3, vb3)
    sweep(c3, va3, f3, vb3, 3, 1, 0, NZ3)
    sweep(c3, vb3, f3, va3, 3, 1, 0, NZ3)
    sweep(c3, va3, f3, vb3, 3, 1, 0, NZ3)
    sweep(c3, vb3, f3, va3, 3, 1, 0, NZ3)
    sweep(c3, va3, f3, vb3, 3, 1, 0, NZ3)

    widen(vb3, wide3, 1, 0, NZ3)
    add_coarse(vb2, wide3, 1, 1, 0, NZ2, 0)
    sweep(c2, vb2, f2, va2, 2, 1, 0, NZ2)
    sweep(c2, va2, f2, vb2, 2, 1, 0, NZ2)

    lo1, hi1 = HALO1 - 8, HALO1 + OWN1 + 8
    widen(vb2, wide2, 1, lo1 // 2, (hi1 - lo1) // 2)
    add_coarse(vb1, wide2, 2, 2, lo1, hi1, lo1)
    sweep(c1, vb1, f1, va1, 1, 2, lo1, hi1)
    sweep(c1, va1, f1, vb1, 1, 2, lo1, hi1)

    widen(vb1, wide1, 2, HALO1 - HALO0 // 2, 72)
    zero_pads(vb0, fields_of(4), NZ0)
    for copy in copies:
        copy.wait()
    add_coarse(va0, wide1, 4, 2, 0, NZ0, 0)
    sweep(c0, va0, v00, vb0, 0, 4, 0, NZ0, PAD)

    def last(t, held):
        held = list(held)
        rows = span(HALO0 + t)
        for x, y in cells_of(4):
            centres, near = neighbours(c0, vb0, 4, 0, x, y, HALO0 + t)
            done = [
                near[f] + (v00[f, x, y, span(PAD + HALO0 + t), :] + (1.0 - RELAX) * centres[f])
                for f in range(3)
            ]
            for f in range(3):
                va0[f, x, y, span(t), :] = done[f]
            for i in range(3):
                gi = g[i, x, y, rows, :]
                for j in range(3):
                    held[3 * i + j] = held[3 * i + j] + gi * done[j]
        return tuple(held)

    nothing = jnp.zeros((8, LANES), jnp.float32)
    fluxes = over(4, 0, OWN0, last, (nothing,) * 9)

    tensor = jnp.zeros((3, 3), jnp.float32)
    place = [lax.broadcasted_iota(jnp.int32, (3, 3), n) for n in range(2)]
    for i in range(3):
        for j in range(3):
            part = fluxes[3 * i + j]
            if i == j:
                part = part + diag[i, :, :]
            whole = jnp.sum(jnp.sum(part, axis=0, keepdims=True), axis=1, keepdims=True)
            tensor = jnp.where((place[0] == i) & (place[1] == j), whole, tensor)
    tensor = tensor * share
    for n in range(sums.shape[0]):
        sums[n, :, :] = tensor

    start = lax.axis_index("row") * 32 + lax.axis_index("col") * 4
    for f in range(3):
        for t in range(0, OWN0, 8):
            block = nothing
            for x, y in cells_of(4):
                amount = (32 * x + 4 * y + LANES - start) & (LANES - 1)
                piece = pltpu.roll(va0[f, x, y, span(t), :], amount, 1)
                block = jnp.where((lane & 0b1101100) == 32 * x + 4 * y, piece, block)
            mixed[span(t), :] = block
        block = mixed[...].T
        for x in range(8):
            for ylo in range(4):
                begin = (x % 4) * 32 + (x // 4) * 16 + ylo * 4
                p[f, x, pl.ds(ylo, 4, stride=4), :] = block[begin : begin + 4]


def f32(*shape):
    return jax.ShapeDtypeStruct(shape, jnp.float32)


def scratch(*shape):
    return pltpu.VMEM(shape, jnp.float32)


def level_scratch(side, nz, last=False):
    rows = nz + 2 * PAD
    got = [scratch(side, side, rows, LANES)] * 4
    got += [scratch(6, side, side, nz, LANES), scratch(3, side, side, nz, LANES)]
    if not last:
        got += [scratch(side, side, nz, LANES), scratch(3, side, side, nz + 8, LANES)]
    return got + [scratch(3, side, side, rows, LANES)] * 2


def params():
    return pltpu.CompilerParams(vmem_limit_bytes=VMEM_LIMIT)


VM = pl.BlockSpec(memory_space=pltpu.VMEM)
SM = pl.BlockSpec(memory_space=pltpu.SMEM)
HB = pl.BlockSpec(memory_space=pl.ANY)
ROWS0 = NZ0 + 2 * PAD


def conductivities(labels, table):
    return pl.pallas_call(
        look_up,
        out_shape=[f32(LANES, LANES), f32(HALO0, LANES), f32(HALO0, LANES)],
        in_specs=[VM, SM],
        out_specs=[VM] * 3,
        scratch_shapes=[scratch(LANES, LANES)],
        name="look_up",
    )(labels, table)


def down(blocks):
    return pl.pallas_call(
        down_kernel,
        out_shape=[
            f32(6, 4, 4, NZ0, LANES), f32(3, 4, 4, ROWS0, LANES), f32(3, 4, 4, ROWS0, LANES),
            f32(3, 4, 4, NZ0, LANES), f32(4, 2, 2, OWN1, LANES), f32(4, 2, 2, HALO1, LANES),
            f32(4, 2, 2, HALO1, LANES), f32(3, 8, LANES),
        ],
        in_specs=[VM],
        out_specs=[HB] * 4 + [VM] * 4,
        scratch_shapes=[scratch(4, 4, ROWS0, LANES)] * 4
        + [
            scratch(6, 4, 4, NZ0, LANES), scratch(3, 4, 4, NZ0, LANES), scratch(4, 4, NZ0, LANES),
            scratch(3, 4, 4, NZ0, LANES),
            scratch(3, 4, 4, ROWS0, LANES), scratch(3, 4, 4, ROWS0, LANES),
            pltpu.SemaphoreType.DMA((4,)),
        ],
        compiler_params=params(),
        name="down",
    )(blocks)


def up(c0, v00, v01, g, own, below, above, diag, depth, cells):
    return pl.pallas_call(
        functools.partial(up_kernel, 1.0 / cells),
        out_shape=[f32(3, 8, 16, LANES), f32(depth, 3, 3)],
        in_specs=[HB] * 4 + [VM] * 4,
        out_specs=[VM] * 2,
        scratch_shapes=level_scratch(2, NZ1) + level_scratch(1, NZ2) + level_scratch(1, NZ3, True)
        + [
            scratch(3, 2, 2, 144, LANES), scratch(3, 1, 1, 80, LANES), scratch(3, 1, 1, 80, LANES),
            scratch(3, 4, 4, ROWS0, LANES), scratch(3, 4, 4, ROWS0, LANES),
            scratch(6, 4, 4, NZ0, LANES), scratch(3, 4, 4, ROWS0, LANES), scratch(3, 4, 4, NZ0, LANES),
            scratch(LANES, LANES), pltpu.SemaphoreType.DMA((4,)),
        ],
        compiler_params=params(),
        name="up",
    )(c0, v00, v01, g, own, below, above, diag)


def from_below(x):
    n = lax.axis_size("dep")
    return lax.ppermute(x, "dep", [(i, i + 1) for i in range(n - 1)])


def from_above(x):
    n = lax.axis_size("dep")
    return lax.ppermute(x, "dep", [(i + 1, i) for i in range(n - 1)])


def body(labels, conductivity):
    k, high, low = conductivities(labels, conductivity)
    column = jnp.concatenate([from_below(high), k, from_above(low)], axis=0)
    plane = lax.axis_size("row") * lax.axis_size("col")
    blocks = lax.all_to_all(
        jnp.broadcast_to(column[None], (plane,) + column.shape), ("row", "col"), 0, 0
    )
    c0, v00, v01, g, own, low, high, diag = down(blocks)
    above = from_above(low)
    below = from_below(high)
    depth = lax.axis_size("dep")
    cells = plane * labels.size * depth
    p, sums = up(c0, v00, v01, g, own, below, above, diag, depth, cells)
    parts = lax.all_to_all(sums, "dep", 0, 0)
    tensor = jnp.sum(parts, axis=0)
    return p, tensor


def solution(mesh):
    in_specs = (P("row", "col", "dep"), P())
    out_specs = (P(None, "row", "col", "dep"), P())
    return jax.shard_map(body, mesh=mesh, in_specs=in_specs, out_specs=out_specs, check_vma=False)
```
